512 devices in a mesh: dp: 4 (over y), wide: 32 (over x, z_lo, core), narrow: 4 (over z_hi).
Axes of the slice: x: 4, y: 4, z: 16 (z_hi: 4, z_lo: 4; z = z_hi * 4 + z_lo), core: 2. Of those that a mesh axis runs over, the one named last changes fastest.
Arguments:
- tokens: bfloat16 [16384, 1024], P(('wide', 'narrow')), may hold values from -6 to 6
- route: int32 [16384], P(('wide', 'narrow')), may hold values from 0 to 63, as said below
- slot: int32 [16384], P(('wide', 'narrow')), may hold values from 0 to 2, as said below
- gate: float32 [16384], P(('wide', 'narrow')), may hold values from 0.3 to 1
- w_in: bfloat16 [128, 1024, 2048], P(('wide', 'narrow'), None, 'dp'), may hold values from -0.1875 to 0.1875
- w_out: bfloat16 [128, 2048, 1024], P(('wide', 'narrow'), 'dp'), may hold values from -0.09375 to 0.09375
- cotangent: bfloat16 [16384, 1024], P(('wide', 'narrow')), may hold values from -6 to 6
Outputs:
- mixed: bfloat16 [16384, 1024], P(('wide', 'narrow'))
- input_grad: bfloat16 [16384, 1024], P(('wide', 'narrow'))
- grad_in: bfloat16 [128, 1024, 2048], P(('wide', 'narrow'), None, 'dp')
The draws below stay inside these ranges and needn't reach their ends.
Inputs may be any that keep to these rules, and one draw needn't show every extreme that they name: `route`: within each aligned block of 128 rows each expert is named at most 3 times; one expert is named exactly 3 times in every block. Within each aligned block of 128 rows the pairs (route, slot) are all different.
All inputs are finite; a program needn't handle non-finite values.
Results may differ from the reference program's by a relative error of at most 0.0057.
Values may be sent and summed in bfloat16 or wider, within the bound.
A program may use at most 64 MiB of HBM per device.

```python
import jax
import jax.numpy as jnp
from jax import lax

D = 1024
EH = 4096
TOK_DEV = 128
EXPERTS = 64
CAP = 3
TOKENS = 16384


def route_cells(key):
    blocks = TOKENS // TOK_DEV
    cells = EXPERTS * CAP
    full = jax.random.randint(jax.random.fold_in(key, 11), (), 0, EXPERTS)

    def one_block(block):
        sub = jax.random.fold_in(key, block + 100)
        order = jax.random.permutation(jax.random.fold_in(sub, 1), cells)
        ranking = jnp.argsort(order).astype(jnp.int32)
        index = jnp.arange(cells, dtype=jnp.int32)
        score = jnp.where(index // CAP == full, index % CAP - CAP, ranking)
        chosen = jnp.argsort(score)[:TOK_DEV].astype(jnp.int32)
        mixing = jax.random.permutation(jax.random.fold_in(sub, 2), TOK_DEV)
        return chosen[mixing]
    return jax.vmap(one_block)(jnp.arange(blocks, dtype=jnp.int32)).reshape(TOKENS)


def draw_route(key, part):
    return (route_cells(key) // CAP).astype(jnp.int32)


def draw_slot(key, part):
    return (route_cells(key) % CAP).astype(jnp.int32)


def level_of(rng, shape, split, low, high):
    loudness, own = 1.0, jax.random.fold_in(rng, 6)
    for axis_at, parts in split:
        draws = jnp.exp(jax.random.uniform(jax.random.fold_in(own, axis_at), (parts,), jnp.float32, low / len(split), high / len(split)))
        loudness = loudness * jnp.repeat(draws, shape[axis_at] // parts).reshape([-1 if axis == axis_at else 1 for axis in range(len(shape))])
    return loudness


def noise(rng, dims, width, limit, split=(), kind=jnp.bfloat16):
    result = width * jax.random.normal(rng, dims, jnp.float32)
    if split:
        result = result * level_of(rng, dims, split, -0.22, 0.18)
    return jnp.clip(result, -limit, limit).astype(kind)


def setup_inputs(seed: int = 0) -> dict:
    seeds = jax.random.split(jax.random.key(seed), 8)
    return {
        "tokens": noise(seeds[0], (TOKENS, D), 1.0, 6.0, ((0, 128),)),
        "route": draw_route(jax.random.fold_in(seeds[7], 71), 0),
        "slot": draw_slot(jax.random.fold_in(seeds[7], 71), 0),
        "gate": jnp.clip(0.3 + 0.7 * jax.random.uniform(seeds[3], (TOKENS,), jnp.float32) ** level_of(seeds[3], (TOKENS,), ((0, 128),), -0.2, 0.2), 0.3, 1.0),
        "w_in": noise(seeds[4], (2 * EXPERTS, D, EH // 2), D ** -0.5, 0.1875, ((0, 128), (2, 4))),
        "w_out": noise(seeds[5], (2 * EXPERTS, EH // 2, D), EH ** -0.5, 0.09375, ((0, 128), (1, 4))),
        "cotangent": noise(seeds[6], (TOKENS, D), 1.0, 6.0, ((0, 128),)),
    }


def gelu_pair(hidden, upstream):
    active, back = jax.vjp(lambda value: jax.nn.gelu(value, approximate=True), hidden)
    return (active.astype(jnp.bfloat16), back(upstream)[0].astype(jnp.bfloat16))

def expert_pass(rows, halves_in, halves_out):
    weight_in = jnp.concatenate([halves_in[0], halves_in[1]], axis=1)
    weight_out = jnp.concatenate([halves_out[0], halves_out[1]], axis=0)
    xs = rows[:, :D]
    gs = rows[:, D:]
    hidden = jnp.dot(xs, weight_in, preferred_element_type=jnp.float32)
    upstream = jnp.dot(gs, weight_out.T, preferred_element_type=jnp.float32)
    active, delta = gelu_pair(hidden, upstream)
    out_rows = jnp.dot(active, weight_out, preferred_element_type=jnp.float32).astype(jnp.bfloat16)
    back_rows = jnp.dot(delta, weight_in.T, preferred_element_type=jnp.float32).astype(jnp.bfloat16)
    grad_full = jnp.dot(xs.T, delta, preferred_element_type=jnp.float32).astype(jnp.bfloat16)
    half = EH // 2
    grad_in = jnp.stack([grad_full[:, :half], grad_full[:, half:]], axis=0)
    return (jnp.concatenate([out_rows, back_rows], axis=1), grad_in)

def reference(tokens, route, slot, gate, w_in, w_out, cotangent):
    scaled = (gate[:, None] * cotangent.astype(jnp.float32)).astype(jnp.bfloat16)
    packed = jnp.concatenate([tokens, scaled], axis=1)
    sources = TOKENS // TOK_DEV
    block = (jnp.arange(TOKENS, dtype=jnp.int32) // TOK_DEV).astype(jnp.int32)
    position = (block * CAP + slot).astype(jnp.int32)
    buffers = jnp.zeros((EXPERTS, sources * CAP, 2 * D), jnp.bfloat16).at[route, position].set(packed)
    paired_in = w_in.reshape(EXPERTS, 2, D, EH // 2)
    paired_out = w_out.reshape(EXPERTS, 2, EH // 2, D)
    results, grad_in = lax.map(lambda item: expert_pass(item[0], item[1], item[2]), (buffers, paired_in, paired_out))
    picked = results[route, position].astype(jnp.float32)
    mixed = (tokens.astype(jnp.float32) + gate[:, None] * picked[:, :D]).astype(jnp.bfloat16)
    input_grad = (cotangent.astype(jnp.float32) + picked[:, D:]).astype(jnp.bfloat16)
    return (mixed, input_grad, grad_in.reshape(2 * EXPERTS, D, EH // 2))
```

```python
import functools

import jax
import jax.numpy as jnp
import numpy as np
from jax import lax
from jax.experimental import pallas as pl
from jax.experimental.pallas import tpu as pltpu
from jax.sharding import PartitionSpec as P

F32 = jnp.float32
BF16 = jnp.bfloat16
MESH = pl.DeviceIdType.MESH
CAP = 3
NX, NZL, NC, NZH, NY = 4, 4, 2, 4, 4
GROUP = 4
LANES = 128


def dims():
    nq, nz = NX * NC, NZL * NZH
    return nq, nz, nz // 2


def offsets(nz):
    order = [0]
    for step in range(1, nz // 2):
        order += [step, nz - step]
    return order + [nz // 2]


def regroup_tables():
    nq, nz, nk = dims()
    into = np.zeros((nk, nq, CAP, nq, nk, CAP), np.float32)
    back = np.zeros((nq, nk, CAP, nz, nq, CAP), np.float32)
    for q in range(nq):
        for s in range(CAP):
            for k in range(nk):
                into[k, q, s, q, k, s] = 1
            for z in range(nz):
                k = z // (2 * NZL) * NZL + z % NZL
                back[q, k, s, z, q, s] = 1
    cells = nq * nk * CAP
    return into.reshape(cells, cells), back.reshape(cells, nz * nq * CAP)


def to_message(value):
    parts = [value[:, b * LANES : (b + 1) * LANES] for b in range(4)]
    return jnp.concatenate(parts, axis=0).astype(BF16)


def block_of(messages, rows, b):
    parts = [messages[i, b * rows : (b + 1) * rows] for i in range(messages.shape[0])]
    return jnp.concatenate(parts, axis=0)


def from_messages(messages, rows):
    wide = messages.astype(F32)
    return jnp.concatenate([block_of(wide, rows, b) for b in range(4)], axis=1).astype(BF16)


def trailing(left, right):
    return lax.dot_general(left, right, (((1,), (1,)), ((), ())), preferred_element_type=F32)


def leading(left, right):
    return lax.dot_general(left, right, (((0,), (0,)), ((), ())), preferred_element_type=F32)


def gelu_pair(hidden, upstream):
    scale, cubic = 0.7978845608, 0.044715
    square = hidden * hidden
    bent = jnp.tanh(scale * hidden * (1.0 + cubic * square))
    half = 0.5 * (1.0 + bent)
    active = hidden * half
    slope = half + 0.5 * hidden * (1.0 - bent * bent) * (scale * (1.0 + 3.0 * cubic * square))
    return active.astype(BF16), (slope * upstream).astype(BF16)


def kernel(
    route_ref, slot_ref, gate_ref, tok_ref, cot_ref, win_hbm, wout_hbm, into_ref, back_ref,
    mixed_ref, ig_ref, grad_ref,
    win, wout, table, s1_send, s1_recv, s2_send, xr, xs_buf, delta_buf, prt, rsa, rsp, rsm, mrg,
    z_send, z_recv, s6_send, s6_recv, ob,
    w_sem, s1_ss, s1_rs, z_ss, z_rs, ag_ss, ag_rs, rs_ss, rs_rs, zb_ss, zb_rs, s6_ss, s6_rs, ob_ss, ob_rs,
):
    nq, nz, nk = dims()
    order = offsets(nz)
    rows = nk * CAP
    tokens, width = tok_ref.shape
    quarter = width // NY
    groups = nz // GROUP
    half = GROUP // 2
    cells = nq * nk * CAP

    y = lax.axis_index("dp")
    w = lax.axis_index("wide")
    zh = lax.axis_index("narrow")
    c = lax.rem(w, NC)
    zl = lax.rem(w // NC, NZL)
    x = w // (NC * NZL)
    q = x * NC + c
    z = zh * NZL + zl
    yp, ym, yo = lax.rem(y + 1, NY), lax.rem(y + NY - 1, NY), lax.rem(y + 2, NY)

    def at_q(other):
        return (y, (other // NC * NZL + zl) * NC + lax.rem(other, NC), zh)

    def at_z(other):
        return (y, (x * NZL + lax.rem(other, NZL)) * NC + c, other // NZL)

    def at_y(other):
        return (other, w, zh)

    def k_of(other):
        return other // (2 * NZL) * NZL + lax.rem(other, NZL)

    barrier = pltpu.get_barrier_semaphore()
    peers = [at_q(lax.rem(q + d, nq)) for d in range(1, nq)]
    peers += [at_z(lax.rem(z + d, nz)) for d in range(1, nz)]
    peers += [at_y(yp), at_y(ym)]
    for peer in peers:
        pl.semaphore_signal(barrier, inc=1, device_id=peer, device_id_type=MESH)

    load_in = pltpu.make_async_copy(win_hbm.at[0], win, w_sem.at[0])
    load_out = pltpu.make_async_copy(wout_hbm.at[0], wout, w_sem.at[1])
    load_in.start()
    load_out.start()

    pending = []

    def send(src, dst, send_sem, recv_sem, peer):
        copy = pltpu.make_async_remote_copy(
            src_ref=src, dst_ref=dst, send_sem=send_sem, recv_sem=recv_sem,
            device_id=peer, device_id_type=MESH,
        )
        copy.start()
        pending.append(copy)

    def arrived(dst, sem):
        pltpu.make_async_remote_copy(
            src_ref=dst, dst_ref=dst, send_sem=sem, recv_sem=sem, device_id=at_y(y), device_id_type=MESH
        ).wait_recv()

    expert = route_ref[...]
    per_c = NZH // 2
    e_ph = lax.rem(expert, per_c)
    e_w = lax.div(expert, per_c)
    e_c = lax.rem(e_w, NC)
    e_zl = lax.rem(lax.div(e_w, NC), NZL)
    e_x = lax.div(e_w, NC * NZL)
    cell = ((e_x * NC + e_c) * nk + e_ph * NZL + e_zl) * CAP + slot_ref[...]
    ids = lax.broadcasted_iota(jnp.int32, (cells, tokens), 0)
    table[...] = jnp.where(ids == cell, 1.0, 0.0).astype(BF16)

    gates = jnp.transpose(jnp.broadcast_to(gate_ref[...], (LANES, tokens)))
    gates = jnp.concatenate([gates] * (quarter // LANES), axis=1)
    mine = pl.ds(pl.multiple_of(y * quarter, quarter), quarter)
    scaled = (gates * cot_ref[:, mine].astype(F32)).astype(BF16)
    packed = jnp.concatenate([tok_ref[:, mine], scaled], axis=1)
    outgoing = jnp.dot(table[...], packed, preferred_element_type=F32)
    for other in range(nq):
        s1_send[other] = to_message(outgoing[other * rows : (other + 1) * rows])

    pl.semaphore_wait(barrier, len(peers))

    for d in range(1, nq):
        other = lax.rem(q + d, nq)
        send(s1_send.at[other], s1_recv.at[q], s1_ss.at[d], s1_rs.at[d], at_q(other))
    s1_recv[q] = s1_send[q]
    for d in range(1, nq):
        arrived(s1_recv.at[lax.rem(q + nq - d, nq)], s1_rs.at[d])

    sorted_rows = jnp.dot(into_ref[...], from_messages(s1_recv[...], rows), preferred_element_type=F32)
    for k in range(nk):
        s2_send[k] = to_message(sorted_rows[k * rows : (k + 1) * rows])
    for i in range(1, nz):
        other = lax.rem(z + order[i], nz)
        send(s2_send.at[k_of(other)], xr.at[y, i], z_ss.at[i], z_rs.at[i], at_z(other))
    xr[y, 0] = s2_send[k_of(z)]

    def gather(g):
        for i in range(g * GROUP, (g + 1) * GROUP):
            if i > 0:
                arrived(xr.at[y, i], z_rs.at[i])
            send(xr.at[y, i], xr.at[y, i], ag_ss.at[0, i], ag_rs.at[0, i], at_y(yp))
            send(xr.at[y, i], xr.at[y, i], ag_ss.at[1, i], ag_rs.at[1, i], at_y(ym))

    def relay(g):
        for i in range(g * GROUP, (g + 1) * GROUP):
            if i % 2 == 0:
                arrived(xr.at[ym, i], ag_rs.at[0, i])
                send(xr.at[ym, i], xr.at[ym, i], ag_ss.at[2, i], ag_rs.at[2, i], at_y(yp))
            else:
                arrived(xr.at[yp, i], ag_rs.at[1, i])
                send(xr.at[yp, i], xr.at[yp, i], ag_ss.at[2, i], ag_rs.at[2, i], at_y(ym))

    def compute(g):
        first = g * GROUP
        for i in range(first, first + GROUP):
            if i % 2 == 0:
                arrived(xr.at[yp, i], ag_rs.at[1, i])
            else:
                arrived(xr.at[ym, i], ag_rs.at[0, i])
            arrived(xr.at[yo, i], ag_rs.at[2, i])
        lot = GROUP * rows
        here = pl.ds(g * lot, lot)
        blocks = []
        for part in range(NY):
            messages = xr[part, first : first + GROUP].astype(F32)
            blocks.append([block_of(messages, rows, b).astype(BF16) for b in range(4)])
        xs = jnp.concatenate([b for four in blocks for b in four[:2]], axis=1)
        gs = jnp.concatenate([b for four in blocks for b in four[2:]], axis=1)
        xs_buf[here, :] = xs
        hidden = jnp.dot(xs, win[...], preferred_element_type=F32)
        active, delta = gelu_pair(hidden, trailing(gs, wout[...]))
        delta_buf[here, :] = delta
        out = jnp.dot(active, wout[...], preferred_element_type=F32)
        back = trailing(delta, win[...])
        for part in range(NY):
            cols = slice(part * quarter, (part + 1) * quarter)
            both = jnp.concatenate([out[:, cols], back[:, cols]], axis=1)
            for j in range(GROUP):
                prt[part, first + j] = to_message(both[j * rows : (j + 1) * rows])

    def scatter(g):
        a, b = pl.ds(g * GROUP, half), pl.ds(g * GROUP + half, half)
        send(prt.at[yo, a], rsa.at[0, g], rs_ss.at[0, g], rs_rs.at[0, g], at_y(yp))
        send(prt.at[yo, b], rsa.at[1, g], rs_ss.at[1, g], rs_rs.at[1, g], at_y(ym))
        send(prt.at[yp, b], rsp.at[0, g], rs_ss.at[2, g], rs_rs.at[2, g], at_y(yp))
        send(prt.at[ym, a], rsp.at[1, g], rs_ss.at[3, g], rs_rs.at[3, g], at_y(ym))

    def merge(g):
        a, b = pl.ds(g * GROUP, half), pl.ds(g * GROUP + half, half)
        arrived(rsa.at[0, g], rs_rs.at[0, g])
        mrg[0, g] = (rsa[0, g].astype(F32) + prt[yp, a].astype(F32)).astype(BF16)
        send(mrg.at[0, g], rsm.at[0, g], rs_ss.at[4, g], rs_rs.at[4, g], at_y(yp))
        arrived(rsa.at[1, g], rs_rs.at[1, g])
        mrg[1, g] = (rsa[1, g].astype(F32) + prt[ym, b].astype(F32)).astype(BF16)
        send(mrg.at[1, g], rsm.at[1, g], rs_ss.at[5, g], rs_rs.at[5, g], at_y(ym))

    def finish(g):
        a, b = pl.ds(g * GROUP, half), pl.ds(g * GROUP + half, half)
        arrived(rsp.at[0, g], rs_rs.at[2, g])
        arrived(rsp.at[1, g], rs_rs.at[3, g])
        arrived(rsm.at[0, g], rs_rs.at[4, g])
        arrived(rsm.at[1, g], rs_rs.at[5, g])
        z_send[a] = (prt[y, a].astype(F32) + rsm[0, g].astype(F32) + rsp[1, g].astype(F32)).astype(BF16)
        z_send[b] = (prt[y, b].astype(F32) + rsp[0, g].astype(F32) + rsm[1, g].astype(F32)).astype(BF16)
        for i in range(g * GROUP, (g + 1) * GROUP):
            if i == 0:
                z_recv[z] = z_send[0]
            else:
                other = lax.rem(z + nz - order[i], nz)
                send(z_send.at[i], z_recv.at[z], zb_ss.at[i], zb_rs.at[i], at_z(other))

    load_in.wait()
    load_out.wait()
    for g in range(groups + 2):
        if g < groups:
            gather(g)
            relay(g)
        if 0 <= g - 2 < groups:
            merge(g - 2)
        if 0 <= g - 1 < groups:
            compute(g - 1)
            scatter(g - 1)
        if 0 <= g - 2 < groups:
            finish(g - 2)

    slab = min(256, width)
    for first in range(0, width, slab):
        grad_ref[0, first : first + slab, :] = leading(
            xs_buf[:, first : first + slab], delta_buf[...]
        ).astype(BF16)

    for i in range(1, nz):
        arrived(z_recv.at[lax.rem(z + order[i], nz)], zb_rs.at[i])
    returned = jnp.dot(back_ref[...], from_messages(z_recv[...], rows), preferred_element_type=F32)
    for other in range(nq):
        s6_send[other] = to_message(returned[other * rows : (other + 1) * rows])
    for d in range(1, nq):
        other = lax.rem(q + d, nq)
        send(s6_send.at[other], s6_recv.at[q], s6_ss.at[d], s6_rs.at[d], at_q(other))
    s6_recv[q] = s6_send[q]
    for d in range(1, nq):
        arrived(s6_recv.at[lax.rem(q + nq - d, nq)], s6_rs.at[d])

    picked = leading(table[...], from_messages(s6_recv[...], rows))
    ob[y, 0] = (tok_ref[:, mine].astype(F32) + gates * picked[:, :quarter]).astype(BF16)
    ob[y, 1] = (cot_ref[:, mine].astype(F32) + picked[:, quarter:]).astype(BF16)
    send(ob.at[y], ob.at[y], ob_ss.at[0], ob_rs.at[0], at_y(yp))
    send(ob.at[y], ob.at[y], ob_ss.at[1], ob_rs.at[1], at_y(ym))
    arrived(ob.at[ym], ob_rs.at[0])
    send(ob.at[ym, 0], ob.at[ym, 0], ob_ss.at[2], ob_rs.at[2], at_y(yp))
    arrived(ob.at[yp], ob_rs.at[1])
    send(ob.at[yp, 1], ob.at[yp, 1], ob_ss.at[3], ob_rs.at[3], at_y(ym))
    arrived(ob.at[yo, 0], ob_rs.at[2])
    arrived(ob.at[yo, 1], ob_rs.at[3])
    for part in range(NY):
        cols = pl.ds(part * quarter, quarter)
        mixed_ref[:, cols] = ob[part, 0]
        ig_ref[:, cols] = ob[part, 1]
    for copy in pending:
        copy.wait_send()


def shards(tokens, route, slot, gate, w_in, w_out, cotangent):
    nq, nz, nk = dims()
    rows = nk * CAP
    groups = nz // GROUP
    half = GROUP // 2
    count, width = tokens.shape
    hidden = w_in.shape[2]
    into, back = regroup_tables()
    message = (4 * rows, LANES)
    vmem = pl.BlockSpec(memory_space=pltpu.VMEM)
    anywhere = pl.BlockSpec(memory_space=pl.ANY)
    dma = pltpu.SemaphoreType.DMA
    return pl.pallas_call(
        kernel,
        out_shape=(
            jax.ShapeDtypeStruct(tokens.shape, BF16),
            jax.ShapeDtypeStruct(tokens.shape, BF16),
            jax.ShapeDtypeStruct(w_in.shape, BF16),
        ),
        in_specs=[vmem] * 5 + [anywhere] * 2 + [vmem] * 2,
        out_specs=(vmem, vmem, vmem),
        scratch_shapes=[
            pltpu.VMEM(w_in.shape[1:], BF16),
            pltpu.VMEM(w_out.shape[1:], BF16),
            pltpu.VMEM((nq * nk * CAP, count), BF16),
            pltpu.VMEM((nq, *message), BF16),
            pltpu.VMEM((nq, *message), BF16),
            pltpu.VMEM((nk, *message), BF16),
            pltpu.VMEM((NY, nz, *message), BF16),
            pltpu.VMEM((nz * rows, width), BF16),
            pltpu.VMEM((nz * rows, hidden), BF16),
            pltpu.VMEM((NY, nz, *message), BF16),
            pltpu.VMEM((2, groups, half, *message), BF16),
            pltpu.VMEM((2, groups, half, *message), BF16),
            pltpu.VMEM((2, groups, half, *message), BF16),
            pltpu.VMEM((2, groups, half, *message), BF16),
            pltpu.VMEM((nz, *message), BF16),
            pltpu.VMEM((nz, *message), BF16),
            pltpu.VMEM((nq, *message), BF16),
            pltpu.VMEM((nq, *message), BF16),
            pltpu.VMEM((NY, 2, count, width // NY), BF16),
            dma((2,)),
            dma((nq,)),
            dma((nq,)),
            dma((nz,)),
            dma((nz,)),
            dma((3, nz)),
            dma((3, nz)),
            dma((6, groups)),
            dma((6, groups)),
            dma((nz,)),
            dma((nz,)),
            dma((nq,)),
            dma((nq,)),
            dma((4,)),
            dma((4,)),
        ],
        compiler_params=pltpu.CompilerParams(
            collective_id=0, has_side_effects=True, vmem_limit_bytes=40 * 1024 * 1024
        ),
    )(
        route.reshape(1, count),
        slot.reshape(1, count),
        gate.reshape(1, count),
        tokens,
        cotangent,
        w_in,
        w_out,
        jnp.asarray(into, BF16),
        jnp.asarray(back, BF16),
    )


def solution(mesh):
    return jax.shard_map(
        shards,
        mesh=mesh,
        in_specs=(
            P(("wide", "narrow"), None),
            P(("wide", "narrow")),
            P(("wide", "narrow")),
            P(("wide", "narrow")),
            P(("wide", "narrow"), None, "dp"),
            P(("wide", "narrow"), "dp", None),
            P(("wide", "narrow"), None),
        ),
        out_specs=(
            P(("wide", "narrow"), None),
            P(("wide", "narrow"), None),
            P(("wide", "narrow"), None, "dp"),
        ),
        check_vma=False,
    )
```
